32 devices in a mesh: section: 4 (over y, core), seq: 8 (over z, x).
Axes of the slice: x: 2, y: 2, z: 4, core: 2. Of those that a mesh axis runs over, the one named last changes fastest.
Arguments:
- hidden: bfloat16 [2, 1024, 4096], P(None, 'seq'), may hold values from -6 to 6
- queries: bfloat16 [4, 2, 1024, 4096], P('section', None, 'seq'), may hold values from -6 to 6
- gain: float32 [4, 4096], P('section'), may hold values from 0.5 to 2
- key_weight: bfloat16 [4, 4096, 512], P('section'), may hold values from -1 to 1
- value_weight: bfloat16 [4, 4096, 512], P('section'), may hold values from -0.09375 to 0.09375
- tree_ids: int32 [2, 1024], replicated, may hold values from 0 to 3, as said below
- branch_ids: int32 [2, 1024], replicated, may hold values from 0 to 2, as said below
- span_order: int32 [2, 16], replicated, may hold values from 0 to 15, each once within a row
Outputs:
- layer_out: bfloat16 [4, 2, 1024, 4096], P('section', None, 'seq')
The draws below stay inside these ranges and needn't reach their ends.
Inputs may be any that keep to these rules, and one draw needn't show every extreme that they name: `tree_ids`: in each microbatch nondecreasing along the packed positions, every value of 0 to 3 present, each tree a multiple of 16 positions long. `branch_ids`: within each tree the prompt, chosen and rejected positions come in that order, each branch one position or more. `span_order`: each row is a permutation of 0 to 15.
All inputs are finite; a program needn't handle non-finite values.
Results may differ from the reference program's by a relative error of at most 0.02.
Values may be sent and summed in bfloat16 or wider, within the bound.
A program may use at most 128 MiB of HBM per device.

```python
import math
import jax
import jax.numpy as jnp
from jax import lax

D = 4096
HQ = 32
HK = 4
HD = 128
MICRO = 2
SEQ_LEN = 1024
TREES = 4
SPAN = 64
SPANS = 16
N_SECTION = 4


def tree_layout(key):
    tree_rows = []
    branch_rows = []
    for microbatch in range(MICRO):
        micro_key = jax.random.fold_in(jax.random.fold_in(key, 7), microbatch)
        key_cuts, key_prompt, key_answer = jax.random.split(micro_key, 3)
        blocks = SEQ_LEN // 16
        candidates = (jax.random.permutation(key_cuts, blocks - 1) + 1).astype(jnp.int32)
        boundary = jnp.sort(candidates[:TREES - 1]) * 16
        positions = jnp.arange(SEQ_LEN, dtype=jnp.int32)
        tree_of = jnp.sum((positions[:, None] >= boundary[None, :]).astype(jnp.int32), axis=1).astype(jnp.int32)
        starts = jnp.concatenate([jnp.zeros((1,), jnp.int32), boundary.astype(jnp.int32)])
        finish = jnp.concatenate([boundary.astype(jnp.int32), jnp.full((1,), SEQ_LEN, jnp.int32)])
        prompt_part = jax.random.randint(key_prompt, (TREES,), 1, 7).astype(jnp.int32)
        answer_part = jax.random.randint(key_answer, (TREES,), 1, 7).astype(jnp.int32)
        cut_one = starts + (finish - starts) * prompt_part // 8
        cut_two = cut_one + jnp.maximum((finish - cut_one) * answer_part // 8, 1)
        branch_of = (positions >= cut_one[tree_of]).astype(jnp.int32) + (positions >= cut_two[tree_of]).astype(jnp.int32)
        tree_rows.append(tree_of)
        branch_rows.append(branch_of)
    return (jnp.stack(tree_rows), jnp.stack(branch_rows))


def draw_tree_ids(key, part):
    return tree_layout(key)[0]


def draw_branch_ids(key, part):
    return tree_layout(key)[1]


def draw_hidden(key, part):
    noise = jax.random.normal(jax.random.fold_in(key, 21), (MICRO, SEQ_LEN, D), jnp.float32)
    values = jnp.clip(noise, -6.0, 6.0)
    return values.astype(jnp.bfloat16)


def draw_key_weight(key, part):
    noise = jnp.clip(jax.random.normal(jax.random.fold_in(key, 22), (N_SECTION, D, HK * HD), jnp.float32), -6.0, 6.0) * D ** (-0.5)
    values = noise
    return values.astype(jnp.bfloat16)


def draw_queries(key, part):
    noise = jnp.clip(jax.random.normal(jax.random.fold_in(key, 23), (N_SECTION, MICRO, SEQ_LEN, HQ * HD), jnp.float32), -6.0, 6.0)
    values = noise
    return values.astype(jnp.bfloat16)


def level_of(stream_key, dims, shards, smallest, high):
    level, own = 1.0, jax.random.fold_in(stream_key, 6)
    for position, shards_of in shards:
        heights = jnp.exp(jax.random.uniform(jax.random.fold_in(own, position), (shards_of,), jnp.float32, smallest / len(shards), high / len(shards)))
        level = level * jnp.repeat(heights, dims[position] // shards_of).reshape([-1 if axis == position else 1 for axis in range(len(dims))])
    return level


def normal_values(own_key, extent, deviation, most, cuts=(), kind=jnp.bfloat16):
    loudness = level_of(own_key, extent, cuts, -0.22, 0.18) if cuts else 1.0
    array = jax.random.normal(own_key, extent, jnp.float32) * deviation * loudness
    return jnp.minimum(jnp.maximum(array, -most), most).astype(kind)


def setup_inputs(seed: int = 0) -> dict:
    key_of = jax.random.split(jax.random.key(seed), 9)
    hidden = draw_hidden(jax.random.fold_in(key_of[8], 71), 0)
    queries = draw_queries(jax.random.fold_in(key_of[8], 71), 0)
    gain = jnp.clip(jnp.exp(math.log(2.0) - 1.3862944 * jax.random.uniform(key_of[2], (N_SECTION, D), jnp.float32) ** level_of(key_of[2], (N_SECTION, D), ((0, 4),), -0.2, 0.2)), 0.5, 2.0)
    key_weight = draw_key_weight(jax.random.fold_in(key_of[8], 71), 0)
    value_weight = normal_values(key_of[4], (N_SECTION, D, HK * HD), D ** -0.5, 0.09375, ((0, 4),))
    tree_ids = draw_tree_ids(jax.random.fold_in(key_of[8], 71), 0)
    branch_ids = draw_branch_ids(jax.random.fold_in(key_of[8], 71), 0)
    span_order = jax.vmap(lambda own: jax.random.permutation(own, SPANS))(jax.random.split(key_of[7], MICRO)).reshape((MICRO, SPANS)).astype(jnp.int32)
    return dict(hidden=hidden, queries=queries, gain=gain, key_weight=key_weight, value_weight=value_weight, tree_ids=tree_ids, branch_ids=branch_ids, span_order=span_order)


rope_base = 500000.0

def frequencies():
    exponent = jnp.arange(HD // 2, dtype=jnp.float32) * (2.0 / HD)
    return jnp.power(jnp.float32(rope_base), -exponent)

def rotate(vectors, angles):
    half_dim = vectors.shape[-1] // 2
    cosine = jnp.cos(angles)[..., None, :]
    sine_part = jnp.sin(angles)[..., None, :]
    lower_half = vectors[..., :half_dim]
    upper_half = vectors[..., half_dim:]
    return jnp.concatenate([lower_half * cosine - upper_half * sine_part, upper_half * cosine + lower_half * sine_part], axis=-1)

def tree_positions(tree_ids, branch_ids):
    positions = jnp.arange(tree_ids.shape[1], dtype=jnp.int32)[None, :]
    opening = jnp.concatenate([jnp.ones_like(tree_ids[:, :1]), (tree_ids[:, 1:] != tree_ids[:, :-1]).astype(jnp.int32)], axis=1)
    starts = lax.cummax(jnp.where(opening > 0, positions, 0).astype(jnp.int32), axis=1)
    chosen = (branch_ids == 1).astype(jnp.int32)
    counted = jnp.cumsum(chosen, axis=1, dtype=jnp.int32)
    before = jnp.take_along_axis(counted - chosen, starts, axis=1)
    skipped = jnp.where(branch_ids == 2, counted - before, 0)
    return (positions - starts - skipped).astype(jnp.int32)

def attend(turned, key_rows, value_rows, allowed):
    ratio = HQ // HK
    scale = 1.0 / math.sqrt(HD)
    grouped = turned.reshape(SEQ_LEN, HK, ratio, HD).transpose(1, 0, 2, 3)

    def one_group(operands):
        query_head, key_head, value_head = operands
        scores = jnp.einsum('qgd,kd->gqk', query_head.astype(jnp.float32), key_head.astype(jnp.float32)) * scale
        masked = jnp.where(allowed[None], scores, -jnp.inf)
        row_top = lax.optimization_barrier(jnp.max(masked, axis=-1, keepdims=True))
        weights = jnp.exp(masked - row_top)
        denominator = lax.optimization_barrier(jnp.sum(weights, axis=-1))
        rounded = lax.optimization_barrier(weights.astype(jnp.bfloat16))
        summed = jnp.einsum('gqk,kd->qgd', rounded.astype(jnp.float32), value_head.astype(jnp.float32))
        return summed / denominator.T[..., None]
    per_head = lax.map(one_group, (grouped, key_rows.transpose(1, 0, 2), value_rows.transpose(1, 0, 2)))
    return per_head.transpose(1, 0, 2, 3).reshape(SEQ_LEN, HQ * HD)

def layer(current, query_rows, gain_row, key_mat, value_mat, rotary_pos, allowed):
    widened = current.astype(jnp.float32)
    norm_scale = lax.rsqrt(lax.optimization_barrier(jnp.mean(widened * widened, axis=-1, keepdims=True)) + 1e-05)
    normed = (widened * norm_scale * gain_row).astype(jnp.bfloat16)
    angles = rotary_pos.astype(jnp.float32)[:, None] * frequencies()
    key_proj = jnp.dot(normed, key_mat, preferred_element_type=jnp.float32).reshape(SEQ_LEN, HK, HD)
    key_rows = rotate(key_proj, angles).astype(jnp.bfloat16)
    value_rows = jnp.dot(normed, value_mat, preferred_element_type=jnp.float32).astype(jnp.bfloat16).reshape(SEQ_LEN, HK, HD)
    turned = rotate(query_rows.astype(jnp.float32).reshape(SEQ_LEN, HQ, HD), angles).astype(jnp.bfloat16)
    attended = attend(turned, key_rows, value_rows, allowed).astype(jnp.bfloat16)
    return (widened + attended.astype(jnp.float32)).astype(jnp.bfloat16)

def reference(hidden, queries, gain, key_weight, value_weight, tree_ids, branch_ids, span_order):
    stored_ids = jnp.arange(SEQ_LEN, dtype=jnp.int32)
    packed_all = jnp.take(span_order, stored_ids // SPAN, axis=1).astype(jnp.int32) * SPAN + stored_ids % SPAN
    rotary_all = tree_positions(tree_ids, branch_ids)
    layers = []
    current = hidden
    for section_id in range(N_SECTION):
        results = []
        for microbatch in range(MICRO):
            packed_rows = packed_all[microbatch]
            tree_of = tree_ids[microbatch][packed_rows]
            branch_of = branch_ids[microbatch][packed_rows]
            rotary_pos = rotary_all[microbatch][packed_rows]
            allowed = (tree_of[:, None] == tree_of[None, :]) & (packed_rows[None, :] <= packed_rows[:, None]) & ((branch_of[None, :] == 0) | (branch_of[None, :] == branch_of[:, None]))
            results.append(layer(current[microbatch], queries[section_id, microbatch], gain[section_id], key_weight[section_id], value_weight[section_id], rotary_pos, allowed))
        current = jnp.stack(results)
        layers.append(current)
    return jnp.stack(layers)
```

```python
import functools
import math

import jax
import jax.numpy as jnp
from jax import lax
from jax.experimental import pallas as pl
from jax.experimental.pallas import tpu as pltpu
from jax.sharding import PartitionSpec as P

HQ = 32
HK = 4
HD = 128
SPAN = 64
RATIO = HQ // HK
TILE_HEADS = 4
HIDDEN_AWAY = -1e30
ROPE_BASE = 500000.0
MESH = pl.DeviceIdType.MESH


def kernel(
    sections,
    z_size,
    x_size,
    span_ref,
    rows_ref,
    inverse_ref,
    gain_ref,
    hidden_ref,
    queries_ref,
    key_ref,
    value_ref,
    out_ref,
    state,
    raw,
    turned,
    key_mat,
    value_mat,
    total,
    cosine,
    sine,
    bias,
    kv,
    values,
    result,
    state_sem,
    raw_sem,
    weight_sem,
    next_sem,
    out_sem,
    own_sem,
    pass_sem,
    kv_sem,
):
    section = lax.axis_index("section")
    me = lax.axis_index("seq")
    z = me // x_size
    x = me % x_size
    micro, _, rows, chunk = state.shape
    seq_len = rows_ref.shape[2]
    spans = rows // SPAN
    width = HK * chunk

    @pl.when(section == 0)
    def _():
        for mb in range(micro):
            for c in range(HK):
                pltpu.make_async_copy(
                    hidden_ref.at[mb, :, pl.ds(c * chunk, chunk)],
                    state.at[mb, c],
                    state_sem.at[mb, c],
                ).start()

    def weight_copies(c):
        part = pl.ds(c * chunk, chunk)
        return (
            pltpu.make_async_copy(key_ref.at[0, part], key_mat.at[part], weight_sem.at[0, c]),
            pltpu.make_async_copy(value_ref.at[0, part], value_mat.at[part], weight_sem.at[1, c]),
        )

    for c in range(HK):
        for copy in weight_copies(c):
            copy.start()

    def raw_copy(mb):
        return pltpu.make_async_copy(queries_ref.at[0, mb], raw.at[mb], raw_sem.at[mb])

    for mb in range(micro):
        raw_copy(mb).start()

    barrier = pltpu.get_barrier_semaphore()
    z_peers = [lax.rem(z + d, z_size) * x_size + x for d in range(1, z_size)]
    x_peers = [z * x_size + lax.rem(x + d, x_size) for d in range(1, x_size)]
    for peer in z_peers + x_peers:
        pl.semaphore_signal(barrier, inc=1, device_id=(section, peer), device_id_type=MESH)

    @pl.when(section > 0)
    def _():
        pl.semaphore_signal(barrier, inc=1, device_id=(section - 1, me), device_id_type=MESH)

    @pl.when(section < sections - 1)
    def _():
        pl.semaphore_signal(barrier, inc=1, device_id=(section + 1, me), device_id_type=MESH)

    at_end = (section == 0) | (section == sections - 1)
    peers = len(z_peers) + len(x_peers)

    @pl.when(at_end)
    def _():
        pl.semaphore_wait(barrier, peers + 1)

    @pl.when(jnp.logical_not(at_end))
    def _():
        pl.semaphore_wait(barrier, peers + 2)

    fold = math.log2(math.e) / math.sqrt(HD)
    place = lax.broadcasted_iota(jnp.int32, (rows, 1), 0)
    lanes = lax.broadcasted_iota(jnp.int32, (rows, HD), 1)
    ids = lax.broadcasted_iota(jnp.int32, (rows, seq_len), 1).astype(jnp.float32)

    def count(flags):
        return jnp.sum(jnp.where(flags, 1.0, 0.0), axis=1, keepdims=True)

    for mb in range(micro):
        position = place % SPAN
        for k in range(spans):
            offset = span_ref[mb, me * spans + k] * SPAN
            position = position + jnp.where(place // SPAN == k, offset, 0)
        position = position.astype(jnp.float32)
        tree_row = rows_ref[mb, 0:1, :]
        branch_row = rows_ref[mb, 1:2, :]
        packed_row = rows_ref[mb, 2:3, :]
        code_row = tree_row * 3.0 + branch_row
        here = ids == position
        code = jnp.sum(jnp.where(here, code_row, 0.0), axis=1, keepdims=True)
        tree = jnp.sum(jnp.where(here, tree_row, 0.0), axis=1, keepdims=True)
        first = tree * 3.0
        start = count(code_row < first)
        prompt_end = count(code_row < first + 1.0)
        chosen_end = count(code_row < first + 2.0)
        rejected = (code - first) > 1.5
        gap_from = jnp.where(rejected, prompt_end, 0.0)
        gap_to = jnp.where(rejected, chosen_end, 0.0)
        allowed = (
            (packed_row >= start)
            & (packed_row <= position)
            & ((packed_row < gap_from) | (packed_row >= gap_to))
        )
        bias[mb] = jnp.where(allowed, 0.0, HIDDEN_AWAY)
        angle = (position - start - (gap_to - gap_from)) * inverse_ref[...]
        cosine[mb] = jnp.cos(angle)
        turn = jnp.sin(angle)
        sine[mb] = jnp.where(lanes < HD // 2, -turn, turn)

    values[:, HD:] = jnp.ones((seq_len, HD), jnp.bfloat16)

    def project(mb, first):
        square = jnp.zeros((rows, 1), jnp.float32)
        for c in range(HK):
            if first:
                for copy in weight_copies(c):
                    copy.wait()
            pltpu.make_async_copy(state.at[mb, c], state.at[mb, c], state_sem.at[mb, c]).wait()
            part = pl.ds(c * chunk, chunk)
            wide = state[mb, c].astype(jnp.float32)
            square = square + jnp.sum(wide * wide, axis=1, keepdims=True)
            gained = (wide * gain_ref[:, part]).astype(jnp.bfloat16)
            keys = jnp.dot(gained, key_mat[part, :], preferred_element_type=jnp.float32)
            vals = jnp.dot(gained, value_mat[part, :], preferred_element_type=jnp.float32)
            if c == 0:
                total[0] = keys
                total[1] = vals
            else:
                total[0] += keys
                total[1] += vals
        norm = lax.rsqrt(square * (1.0 / width) + 1e-05)
        for g in range(HK):
            head = pl.ds(g * HD, HD)
            key = total[0, :, head] * norm
            key = key * cosine[mb] + pltpu.roll(key, HD // 2, 1) * sine[mb]
            kv[mb, g, me, :, :HD] = key.astype(jnp.bfloat16)
            kv[mb, g, me, :, HD:] = (total[1, :, head] * norm).astype(jnp.bfloat16)
            for i in range(len(z_peers) + len(x_peers)):
                own_copy(mb, g, i).start()

    def own_copy(mb, g, i):
        peer = (z_peers + x_peers)[i]
        return pltpu.make_async_remote_copy(
            src_ref=kv.at[mb, g, me],
            dst_ref=kv.at[mb, g, me],
            send_sem=own_sem.at[mb, g, i],
            recv_sem=kv_sem.at[mb, g, me],
            device_id=(section, peer),
            device_id_type=MESH,
        )

    def pass_copy(mb, g, i, j):
        return pltpu.make_async_remote_copy(
            src_ref=kv.at[mb, g, z_peers[i]],
            dst_ref=kv.at[mb, g, z_peers[i]],
            send_sem=pass_sem.at[mb, g, i, j],
            recv_sem=kv_sem.at[mb, g, z_peers[i]],
            device_id=(section, x_peers[j]),
            device_id_type=MESH,
        )

    def arrived(mb, g, slot):
        block = kv.at[mb, g, slot]
        pltpu.make_async_copy(block, block, kv_sem.at[mb, g, slot]).wait()

    def hand_on(mb, g):
        for i in range(z_size - 1):
            arrived(mb, g, z_peers[i])
            for j in range(x_size - 1):
                pass_copy(mb, g, i, j).start()

    def all_here(mb, g):
        for d in range(1, x_size):
            for e in range(z_size):
                arrived(mb, g, lax.rem(z + e, z_size) * x_size + lax.rem(x + d, x_size))

    def next_copy(mb, g):
        return pltpu.make_async_remote_copy(
            src_ref=result.at[mb, g],
            dst_ref=state.at[mb, g],
            send_sem=next_sem.at[mb, g],
            recv_sem=state_sem.at[mb, g],
            device_id=(section + 1, me),
            device_id_type=MESH,
        )

    def out_copy(mb, g):
        return pltpu.make_async_copy(
            result.at[mb, g],
            out_ref.at[0, mb, :, pl.ds(pl.multiple_of(g * chunk, chunk), chunk)],
            out_sem.at[mb, g],
        )

    def turn_queries(mb):
        raw_copy(mb).wait()
        spread = cosine[mb] * fold
        cross = sine[mb] * fold

        def group(g, carry):
            for r in range(RATIO):
                h = g * RATIO + r
                query = raw[mb, :, pl.ds(pl.multiple_of(h * HD, HD), HD)].astype(jnp.float32)
                turned[mb, h] = (query * spread + pltpu.roll(query, HD // 2, 1) * cross).astype(
                    jnp.bfloat16
                )
            return carry

        lax.fori_loop(0, HK, group, 0)

    def attend(mb):
        hand_on(mb, 0)

        def group(g, carry):
            @pl.when(g < HK - 1)
            def _():
                hand_on(mb, g + 1)

            all_here(mb, g)
            values[:, :HD] = kv[mb, g, :, :, HD:].reshape(seq_len, HD)
            for t in range(RATIO // TILE_HEADS):
                query = turned[mb, pl.ds(g * RATIO + t * TILE_HEADS, TILE_HEADS)]
                keys = kv[mb, g, :, :, :HD].reshape(seq_len, HD)
                scores = lax.dot_general(
                    query.reshape(TILE_HEADS * rows, HD),
                    keys,
                    (((1,), (1,)), ((), ())),
                    preferred_element_type=jnp.float32,
                )
                scores = scores.reshape(TILE_HEADS, rows, seq_len) + bias[mb]
                top = jnp.max(scores, axis=-1, keepdims=True)
                weights = jnp.exp2(scores - top).astype(jnp.bfloat16)
                summed = jnp.dot(
                    weights.reshape(TILE_HEADS * rows, seq_len),
                    values[...],
                    preferred_element_type=jnp.float32,
                )
                attended = (summed[:, :HD] / summed[:, HD:]).astype(jnp.bfloat16)
                for r in range(TILE_HEADS):
                    part = pl.ds((t * TILE_HEADS + r) * HD, HD)
                    result[mb, g, :, part] = (
                        state[mb, g, :, part].astype(jnp.float32)
                        + attended[r * rows : (r + 1) * rows].astype(jnp.float32)
                    ).astype(jnp.bfloat16)

            @pl.when(section < sections - 1)
            def _():
                next_copy(mb, g).start()

            out_copy(mb, g).start()
            return carry

        lax.fori_loop(0, HK, group, 0)

    @pl.when(section > 0)
    def _():
        for mb in range(micro):
            turn_queries(mb)

    project(0, True)

    @pl.when(section == 0)
    def _():
        for mb in range(1, micro):
            project(mb, False)
        for mb in range(micro):
            turn_queries(mb)

    for mb in range(micro):
        attend(mb)
        if mb + 1 < micro:

            @pl.when(section > 0)
            def _():
                project(mb + 1, False)

    def finish(g, carry):
        for mb in range(micro):
            for i in range(len(z_peers) + len(x_peers)):
                own_copy(mb, g, i).wait_send()
            for i in range(z_size - 1):
                for j in range(x_size - 1):
                    pass_copy(mb, g, i, j).wait_send()
            out_copy(mb, g).wait()

            @pl.when(section < sections - 1)
            def _():
                next_copy(mb, g).wait_send()

        return carry

    lax.fori_loop(0, HK, finish, 0)


def local(sections, z_size, x_size, hidden, queries, gain, key_weight, value_weight, tree_ids,
          branch_ids, span_order):
    micro, rows, width = hidden.shape
    seq_len = tree_ids.shape[1]
    seq = z_size * x_size
    chunk = width // HK
    within = jnp.arange(SPAN, dtype=jnp.int32)
    packed = (span_order[:, :, None] * SPAN + within).reshape(micro, seq_len)
    stacked = jnp.stack([tree_ids, branch_ids, packed], axis=1).astype(jnp.float32)
    exponent = jnp.arange(HD // 2, dtype=jnp.float32) * (2.0 / HD)
    inverse = jnp.power(jnp.float32(ROPE_BASE), -exponent)
    inverse = jnp.concatenate([inverse, inverse])[None]
    vmem = pl.BlockSpec(memory_space=pltpu.VMEM)
    anywhere = pl.BlockSpec(memory_space=pl.ANY)
    half = jnp.bfloat16
    dma = pltpu.SemaphoreType.DMA
    return pl.pallas_call(
        functools.partial(kernel, sections, z_size, x_size),
        out_shape=jax.ShapeDtypeStruct((1, micro, rows, width), half),
        in_specs=[pl.BlockSpec(memory_space=pltpu.SMEM)] + [vmem] * 3 + [anywhere] * 4,
        out_specs=anywhere,
        scratch_shapes=[
            pltpu.VMEM((micro, HK, rows, chunk), half),
            pltpu.VMEM((micro, rows, width), half),
            pltpu.VMEM((micro, HQ, rows, HD), half),
            pltpu.VMEM((width, HK * HD), half),
            pltpu.VMEM((width, HK * HD), half),
            pltpu.VMEM((2, rows, HK * HD), jnp.float32),
            pltpu.VMEM((micro, rows, HD), jnp.float32),
            pltpu.VMEM((micro, rows, HD), jnp.float32),
            pltpu.VMEM((micro, rows, seq_len), jnp.float32),
            pltpu.VMEM((micro, HK, seq, rows, 2 * HD), half),
            pltpu.VMEM((seq_len, 2 * HD), half),
            pltpu.VMEM((micro, HK, rows, chunk), half),
            dma((micro, HK)),
            dma((micro,)),
            dma((2, HK)),
            dma((micro, HK)),
            dma((micro, HK)),
            dma((micro, HK, z_size + x_size - 2)),
            dma((micro, HK, max(z_size - 1, 1), max(x_size - 1, 1))),
            dma((micro, HK, seq)),
        ],
        compiler_params=pltpu.CompilerParams(
            collective_id=0, has_side_effects=True, vmem_limit_bytes=56 * 1024 * 1024
        ),
    )(span_order, stacked, inverse, gain, hidden, queries, key_weight, value_weight)


def solution(mesh):
    seq = mesh.shape["seq"]
    z_size = math.gcd(seq, 4)
    placed = (
        P(None, "seq", None),
        P("section", None, "seq", None),
        P("section", None),
        P("section", None, None),
        P("section", None, None),
        P(),
        P(),
        P(),
    )
    return jax.shard_map(
        functools.partial(local, mesh.shape["section"], z_size, seq // z_size),
        mesh=mesh,
        in_specs=placed,
        out_specs=P("section", None, "seq", None),
        check_vma=False,
    )
```

```python
import functools
import math

import jax
import jax.numpy as jnp
import numpy as np
from jax import lax
from jax.experimental import pallas as pl
from jax.experimental.pallas import tpu as pltpu
from jax.sharding import PartitionSpec as P

HQ = 32
HK = 4
HD = 128
SPAN = 64
RATIO = HQ // HK
TILE_HEADS = 2
HIDDEN_AWAY = -1e30
ROPE_BASE = 500000.0
MESH = pl.DeviceIdType.MESH


def kernel(
    sections,
    z_size,
    x_size,
    span_ref,
    tree_ref,
    branch_ref,
    packed_ref,
    inverse_ref,
    gain_ref,
    hidden_ref,
    queries_ref,
    key_ref,
    value_ref,
    out_ref,
    state,
    raw,
    turned,
    key_mat,
    value_mat,
    total,
    cosine,
    sine,
    bias,
    kv,
    values,
    result,
    state_sem,
    raw_sem,
    weight_sem,
    next_sem,
    out_sem,
    own_sem,
    pass_sem,
    kv_sem,
):
    section = lax.axis_index("section")
    me = lax.axis_index("seq")
    z = me // x_size
    x = me % x_size
    micro, _, rows, chunk = state.shape
    seq_len = tree_ref.shape[1]
    spans = rows // SPAN
    width = HK * chunk

    @pl.when(section == 0)
    def _():
        for mb in range(micro):
            for c in range(HK):
                pltpu.make_async_copy(
                    hidden_ref.at[mb, :, pl.ds(c * chunk, chunk)],
                    state.at[mb, c],
                    state_sem.at[mb, c],
                ).start()

    def weight_copies(c):
        part = pl.ds(c * chunk, chunk)
        return (
            pltpu.make_async_copy(key_ref.at[0, part], key_mat.at[part], weight_sem.at[0, c]),
            pltpu.make_async_copy(value_ref.at[0, part], value_mat.at[part], weight_sem.at[1, c]),
        )

    for c in range(HK):
        for copy in weight_copies(c):
            copy.start()

    def raw_copy(mb):
        return pltpu.make_async_copy(queries_ref.at[0, mb], raw.at[mb], raw_sem.at[mb])

    for mb in range(micro):
        raw_copy(mb).start()

    barrier = pltpu.get_barrier_semaphore()
    z_peers = [lax.rem(z + d, z_size) * x_size + x for d in range(1, z_size)]
    x_peers = [z * x_size + lax.rem(x + d, x_size) for d in range(1, x_size)]
    for peer in z_peers + x_peers:
        pl.semaphore_signal(barrier, inc=1, device_id=(section, peer), device_id_type=MESH)

    @pl.when(section > 0)
    def _():
        pl.semaphore_signal(barrier, inc=1, device_id=(section - 1, me), device_id_type=MESH)

    @pl.when(section < sections - 1)
    def _():
        pl.semaphore_signal(barrier, inc=1, device_id=(section + 1, me), device_id_type=MESH)

    at_end = (section == 0) | (section == sections - 1)
    peers = len(z_peers) + len(x_peers)

    @pl.when(at_end)
    def _():
        pl.semaphore_wait(barrier, peers + 1)

    @pl.when(jnp.logical_not(at_end))
    def _():
        pl.semaphore_wait(barrier, peers + 2)

    fold = math.log2(math.e) / math.sqrt(HD)
    place = lax.broadcasted_iota(jnp.int32, (rows, 1), 0)
    lanes = lax.broadcasted_iota(jnp.int32, (rows, HD), 1)
    ids = lax.broadcasted_iota(jnp.int32, (rows, seq_len), 1).astype(jnp.float32)

    def count(flags):
        return jnp.sum(jnp.where(flags, 1.0, 0.0), axis=1, keepdims=True)

    for mb in range(micro):
        position = place % SPAN
        for k in range(spans):
            offset = span_ref[mb, me * spans + k] * SPAN
            position = position + jnp.where(place // SPAN == k, offset, 0)
        position = position.astype(jnp.float32)
        tree_row = tree_ref[mb : mb + 1, :].astype(jnp.float32)
        branch_row = branch_ref[mb : mb + 1, :].astype(jnp.float32)
        packed_row = packed_ref[mb : mb + 1, :].astype(jnp.float32)
        code_row = tree_row * 3.0 + branch_row
        here = ids == position
        code = jnp.sum(jnp.where(here, code_row, 0.0), axis=1, keepdims=True)
        tree = jnp.sum(jnp.where(here, tree_row, 0.0), axis=1, keepdims=True)
        first = tree * 3.0
        start = count(code_row < first)
        prompt_end = count(code_row < first + 1.0)
        chosen_end = count(code_row < first + 2.0)
        rejected = (code - first) > 1.5
        gap_from = jnp.where(rejected, prompt_end, 0.0)
        gap_to = jnp.where(rejected, chosen_end, 0.0)
        allowed = (
            (packed_row >= start)
            & (packed_row <= position)
            & ((packed_row < gap_from) | (packed_row >= gap_to))
        )
        bias[mb] = jnp.where(allowed, 0.0, HIDDEN_AWAY)
        angle = (position - start - (gap_to - gap_from)) * inverse_ref[...]
        cosine[mb] = jnp.cos(angle)
        turn = jnp.sin(angle)
        sine[mb] = jnp.where(lanes < HD // 2, -turn, turn)

    values[:, HD:] = jnp.ones((seq_len, HD), jnp.bfloat16)

    def project(mb, first):
        square = jnp.zeros((rows, 1), jnp.float32)
        for c in range(HK):
            if first:
                for copy in weight_copies(c):
                    copy.wait()
            pltpu.make_async_copy(state.at[mb, c], state.at[mb, c], state_sem.at[mb, c]).wait()
            part = pl.ds(c * chunk, chunk)
            wide = state[mb, c].astype(jnp.float32)
            square = square + jnp.sum(wide * wide, axis=1, keepdims=True)
            gained = (wide * gain_ref[:, part]).astype(jnp.bfloat16)
            keys = jnp.dot(gained, key_mat[part, :], preferred_element_type=jnp.float32)
            vals = jnp.dot(gained, value_mat[part, :], preferred_element_type=jnp.float32)
            if c == 0:
                total[0] = keys
                total[1] = vals
            else:
                total[0] += keys
                total[1] += vals
        norm = lax.rsqrt(square * (1.0 / width) + 1e-05)
        for g in range(HK):
            head = pl.ds(g * HD, HD)
            key = total[0, :, head] * norm
            key = key * cosine[mb] + pltpu.roll(key, HD // 2, 1) * sine[mb]
            kv[mb, g, me, :, :HD] = key.astype(jnp.bfloat16)
            kv[mb, g, me, :, HD:] = (total[1, :, head] * norm).astype(jnp.bfloat16)
            for i in range(len(z_peers) + len(x_peers)):
                own_copy(mb, g, i).start()

    def own_copy(mb, g, i):
        peer = (z_peers + x_peers)[i]
        return pltpu.make_async_remote_copy(
            src_ref=kv.at[mb, g, me],
            dst_ref=kv.at[mb, g, me],
            send_sem=own_sem.at[mb, g, i],
            recv_sem=kv_sem.at[mb, g, me],
            device_id=(section, peer),
            device_id_type=MESH,
        )

    def pass_copy(mb, g, i, j):
        return pltpu.make_async_remote_copy(
            src_ref=kv.at[mb, g, z_peers[i]],
            dst_ref=kv.at[mb, g, z_peers[i]],
            send_sem=pass_sem.at[mb, g, i, j],
            recv_sem=kv_sem.at[mb, g, z_peers[i]],
            device_id=(section, x_peers[j]),
            device_id_type=MESH,
        )

    def arrived(mb, g, slot):
        block = kv.at[mb, g, slot]
        pltpu.make_async_copy(block, block, kv_sem.at[mb, g, slot]).wait()

    def hand_on(mb, g):
        for i in range(z_size - 1):
            arrived(mb, g, z_peers[i])
            for j in range(x_size - 1):
                pass_copy(mb, g, i, j).start()

    def all_here(mb, g):
        for d in range(1, x_size):
            for e in range(z_size):
                arrived(mb, g, lax.rem(z + e, z_size) * x_size + lax.rem(x + d, x_size))

    def next_copy(mb, g):
        return pltpu.make_async_remote_copy(
            src_ref=result.at[mb, g],
            dst_ref=state.at[mb, g],
            send_sem=next_sem.at[mb, g],
            recv_sem=state_sem.at[mb, g],
            device_id=(section + 1, me),
            device_id_type=MESH,
        )

    def out_copy(mb, g):
        return pltpu.make_async_copy(
            result.at[mb, g],
            out_ref.at[0, mb, :, pl.ds(pl.multiple_of(g * chunk, chunk), chunk)],
            out_sem.at[mb, g],
        )

    def turn_queries(mb):
        raw_copy(mb).wait()
        spread = cosine[mb] * fold
        cross = sine[mb] * fold

        def group(g, carry):
            for r in range(RATIO):
                h = g * RATIO + r
                query = raw[mb, :, pl.ds(pl.multiple_of(h * HD, HD), HD)].astype(jnp.float32)
                turned[mb, h] = (query * spread + pltpu.roll(query, HD // 2, 1) * cross).astype(
                    jnp.bfloat16
                )
            return carry

        lax.fori_loop(0, HK, group, 0)

    def attend(mb):
        hand_on(mb, 0)

        def group(g, carry):
            @pl.when(g < HK - 1)
            def _():
                hand_on(mb, g + 1)

            all_here(mb, g)
            values[:, :HD] = kv[mb, g, :, :, HD:].reshape(seq_len, HD)
            for t in range(RATIO // TILE_HEADS):
                query = turned[mb, pl.ds(g * RATIO + t * TILE_HEADS, TILE_HEADS)]
                keys = kv[mb, g, :, :, :HD].reshape(seq_len, HD)
                scores = lax.dot_general(
                    query.reshape(TILE_HEADS * rows, HD),
                    keys,
                    (((1,), (1,)), ((), ())),
                    preferred_element_type=jnp.float32,
                )
                scores = scores.reshape(TILE_HEADS, rows, seq_len) + bias[mb]
                top = jnp.max(scores, axis=-1, keepdims=True)
                weights = jnp.exp2(scores - top).astype(jnp.bfloat16)
                summed = jnp.dot(
                    weights.reshape(TILE_HEADS * rows, seq_len),
                    values[...],
                    preferred_element_type=jnp.float32,
                )
                attended = (summed[:, :HD] / summed[:, HD:]).astype(jnp.bfloat16)
                for r in range(TILE_HEADS):
                    part = pl.ds((t * TILE_HEADS + r) * HD, HD)
                    result[mb, g, :, part] = (
                        state[mb, g, :, part].astype(jnp.float32)
                        + attended[r * rows : (r + 1) * rows].astype(jnp.float32)
                    ).astype(jnp.bfloat16)

            @pl.when(section < sections - 1)
            def _():
                next_copy(mb, g).start()

            out_copy(mb, g).start()
            return carry

        lax.fori_loop(0, HK, group, 0)

    @pl.when(section > 0)
    def _():
        for mb in range(micro):
            turn_queries(mb)

    project(0, True)

    @pl.when(section == 0)
    def _():
        for mb in range(1, micro):
            project(mb, False)
        for mb in range(micro):
            turn_queries(mb)

    for mb in range(micro):
        attend(mb)
        if mb + 1 < micro:

            @pl.when(section > 0)
            def _():
                project(mb + 1, False)

    def finish(g, carry):
        for mb in range(micro):
            for i in range(len(z_peers) + len(x_peers)):
                own_copy(mb, g, i).wait_send()
            for i in range(z_size - 1):
                for j in range(x_size - 1):
                    pass_copy(mb, g, i, j).wait_send()
            out_copy(mb, g).wait()

            @pl.when(section < sections - 1)
            def _():
                next_copy(mb, g).wait_send()

        return carry

    lax.fori_loop(0, HK, finish, 0)


def local(sections, z_size, x_size, hidden, queries, gain, key_weight, value_weight, tree_ids,
          branch_ids, span_order):
    micro, rows, width = hidden.shape
    seq_len = tree_ids.shape[1]
    seq = z_size * x_size
    chunk = width // HK
    within = jnp.arange(SPAN, dtype=jnp.int32)
    packed = (span_order[:, :, None] * SPAN + within).reshape(micro, seq_len)
    exponent = np.arange(HD // 2, dtype=np.float32) * np.float32(2.0 / HD)
    inverse = np.power(np.float32(ROPE_BASE), -exponent).astype(np.float32)
    inverse = jnp.asarray(np.concatenate([inverse, inverse])[None])
    vmem = pl.BlockSpec(memory_space=pltpu.VMEM)
    anywhere = pl.BlockSpec(memory_space=pl.ANY)
    half = jnp.bfloat16
    dma = pltpu.SemaphoreType.DMA
    return pl.pallas_call(
        functools.partial(kernel, sections, z_size, x_size),
        out_shape=jax.ShapeDtypeStruct((1, micro, rows, width), half),
        in_specs=[pl.BlockSpec(memory_space=pltpu.SMEM)] + [vmem] * 5 + [anywhere] * 4,
        out_specs=anywhere,
        scratch_shapes=[
            pltpu.VMEM((micro, HK, rows, chunk), half),
            pltpu.VMEM((micro, rows, width), half),
            pltpu.VMEM((micro, HQ, rows, HD), half),
            pltpu.VMEM((width, HK * HD), half),
            pltpu.VMEM((width, HK * HD), half),
            pltpu.VMEM((2, rows, HK * HD), jnp.float32),
            pltpu.VMEM((micro, rows, HD), jnp.float32),
            pltpu.VMEM((micro, rows, HD), jnp.float32),
            pltpu.VMEM((micro, rows, seq_len), jnp.float32),
            pltpu.VMEM((micro, HK, seq, rows, 2 * HD), half),
            pltpu.VMEM((seq_len, 2 * HD), half),
            pltpu.VMEM((micro, HK, rows, chunk), half),
            dma((micro, HK)),
            dma((micro,)),
            dma((2, HK)),
            dma((micro, HK)),
            dma((micro, HK)),
            dma((micro, HK, z_size + x_size - 2)),
            dma((micro, HK, max(z_size - 1, 1), max(x_size - 1, 1))),
            dma((micro, HK, seq)),
        ],
        compiler_params=pltpu.CompilerParams(
            collective_id=0, has_side_effects=True, vmem_limit_bytes=56 * 1024 * 1024
        ),
    )(span_order, tree_ids, branch_ids, packed, inverse, gain, hidden, queries, key_weight, value_weight)


def solution(mesh):
    seq = mesh.shape["seq"]
    z_size = math.gcd(seq, 4)
    placed = (
        P(None, "seq", None),
        P("section", None, "seq", None),
        P("section", None),
        P("section", None, None),
        P("section", None, None),
        P(),
        P(),
        P(),
    )
    return jax.shard_map(
        functools.partial(local, mesh.shape["section"], z_size, seq // z_size),
        mesh=mesh,
        in_specs=placed,
        out_specs=P("section", None, "seq", None),
        check_vma=False,
    )
```

```python
import functools
import math

import jax
import jax.numpy as jnp
import numpy as np
from jax import lax
from jax.experimental import pallas as pl
from jax.experimental.pallas import tpu as pltpu
from jax.sharding import PartitionSpec as P

HQ = 32
HK = 4
HD = 128
SPAN = 64
RATIO = HQ // HK
TILE_HEADS = 2
HIDDEN_AWAY = -1e30
ROPE_BASE = 500000.0
MESH = pl.DeviceIdType.MESH


def kernel(
    sections,
    z_size,
    x_size,
    span_ref,
    tree_ref,
    branch_ref,
    packed_ref,
    inverse_ref,
    gain_ref,
    hidden_ref,
    queries_ref,
    key_ref,
    value_ref,
    out_ref,
    state,
    raw,
    turned,
    key_mat,
    value_mat,
    total,
    cosine,
    sine,
    bias,
    kv,
    values,
    result,
    state_sem,
    raw_sem,
    weight_sem,
    next_sem,
    out_sem,
    own_sem,
    pass_sem,
    kv_sem,
):
    section = lax.axis_index("section")
    me = lax.axis_index("seq")
    z = me // x_size
    x = me % x_size
    micro, _, rows, chunk = state.shape
    seq_len = tree_ref.shape[1]
    spans = rows // SPAN
    width = HK * chunk

    @pl.when(section == 0)
    def _():
        for mb in range(micro):
            for c in range(HK):
                pltpu.make_async_copy(
                    hidden_ref.at[mb, :, pl.ds(c * chunk, chunk)],
                    state.at[mb, c],
                    state_sem.at[mb, c],
                ).start()

    def weight_copies(c):
        part = pl.ds(c * chunk, chunk)
        return (
            pltpu.make_async_copy(key_ref.at[0, part], key_mat.at[part], weight_sem.at[0, c]),
            pltpu.make_async_copy(value_ref.at[0, part], value_mat.at[part], weight_sem.at[1, c]),
        )

    for c in range(HK):
        for copy in weight_copies(c):
            copy.start()

    def raw_copy(mb):
        return pltpu.make_async_copy(queries_ref.at[0, mb], raw.at[mb], raw_sem.at[mb])

    for mb in range(micro):
        raw_copy(mb).start()

    barrier = pltpu.get_barrier_semaphore()
    z_peers = [lax.rem(z + d, z_size) * x_size + x for d in range(1, z_size)]
    x_peers = [z * x_size + lax.rem(x + d, x_size) for d in range(1, x_size)]
    for peer in z_peers + x_peers:
        pl.semaphore_signal(barrier, inc=1, device_id=(section, peer), device_id_type=MESH)

    @pl.when(section > 0)
    def _():
        pl.semaphore_signal(barrier, inc=1, device_id=(section - 1, me), device_id_type=MESH)

    @pl.when(section < sections - 1)
    def _():
        pl.semaphore_signal(barrier, inc=1, device_id=(section + 1, me), device_id_type=MESH)

    at_end = (section == 0) | (section == sections - 1)
    peers = len(z_peers) + len(x_peers)

    @pl.when(at_end)
    def _():
        pl.semaphore_wait(barrier, peers + 1)

    @pl.when(jnp.logical_not(at_end))
    def _():
        pl.semaphore_wait(barrier, peers + 2)

    fold = math.log2(math.e) / math.sqrt(HD)
    place = lax.broadcasted_iota(jnp.int32, (rows, 1), 0)
    lanes = lax.broadcasted_iota(jnp.int32, (rows, HD), 1)
    ids = lax.broadcasted_iota(jnp.int32, (rows, seq_len), 1).astype(jnp.float32)

    def count(flags):
        return jnp.sum(jnp.where(flags, 1.0, 0.0), axis=1, keepdims=True)

    def prepare(mb):
        position = place % SPAN
        for k in range(spans):
            offset = span_ref[mb, me * spans + k] * SPAN
            position = position + jnp.where(place // SPAN == k, offset, 0)
        position = position.astype(jnp.float32)
        tree_row = tree_ref[mb : mb + 1, :].astype(jnp.float32)
        branch_row = branch_ref[mb : mb + 1, :].astype(jnp.float32)
        packed_row = packed_ref[mb : mb + 1, :].astype(jnp.float32)
        code_row = tree_row * 3.0 + branch_row
        here = ids == position
        code = jnp.sum(jnp.where(here, code_row, 0.0), axis=1, keepdims=True)
        tree = jnp.sum(jnp.where(here, tree_row, 0.0), axis=1, keepdims=True)
        first = tree * 3.0
        start = count(code_row < first)
        prompt_end = count(code_row < first + 1.0)
        chosen_end = count(code_row < first + 2.0)
        rejected = (code - first) > 1.5
        gap_from = jnp.where(rejected, prompt_end, 0.0)
        gap_to = jnp.where(rejected, chosen_end, 0.0)
        allowed = (
            (packed_row >= start)
            & (packed_row <= position)
            & ((packed_row < gap_from) | (packed_row >= gap_to))
        )
        bias[mb] = jnp.where(allowed, 0.0, HIDDEN_AWAY)
        angle = (position - start - (gap_to - gap_from)) * inverse_ref[...]
        cosine[mb] = jnp.cos(angle)
        turn = jnp.sin(angle)
        sine[mb] = jnp.where(lanes < HD // 2, -turn, turn)

    values[:, HD:] = jnp.ones((seq_len, HD), jnp.bfloat16)

    def project(mb, first):
        square = jnp.zeros((rows, 1), jnp.float32)
        for c in range(HK):
            if first:
                for copy in weight_copies(c):
                    copy.wait()
            pltpu.make_async_copy(state.at[mb, c], state.at[mb, c], state_sem.at[mb, c]).wait()
            part = pl.ds(c * chunk, chunk)
            wide = state[mb, c].astype(jnp.float32)
            square = square + jnp.sum(wide * wide, axis=1, keepdims=True)
            gained = (wide * gain_ref[:, part]).astype(jnp.bfloat16)
            keys = jnp.dot(gained, key_mat[part, :], preferred_element_type=jnp.float32)
            vals = jnp.dot(gained, value_mat[part, :], preferred_element_type=jnp.float32)
            if c == 0:
                total[0] = keys
                total[1] = vals
            else:
                total[0] += keys
                total[1] += vals
        norm = lax.rsqrt(square * (1.0 / width) + 1e-05)
        for g in range(HK):
            head = pl.ds(g * HD, HD)
            key = total[0, :, head] * norm
            key = key * cosine[mb] + pltpu.roll(key, HD // 2, 1) * sine[mb]
            kv[mb, g, me, :, :HD] = key.astype(jnp.bfloat16)
            kv[mb, g, me, :, HD:] = (total[1, :, head] * norm).astype(jnp.bfloat16)
            for i in range(len(z_peers) + len(x_peers)):
                own_copy(mb, g, i).start()

    def own_copy(mb, g, i):
        peer = (z_peers + x_peers)[i]
        return pltpu.make_async_remote_copy(
            src_ref=kv.at[mb, g, me],
            dst_ref=kv.at[mb, g, me],
            send_sem=own_sem.at[mb, g, i],
            recv_sem=kv_sem.at[mb, g, me],
            device_id=(section, peer),
            device_id_type=MESH,
        )

    def pass_copy(mb, g, i, j):
        return pltpu.make_async_remote_copy(
            src_ref=kv.at[mb, g, z_peers[i]],
            dst_ref=kv.at[mb, g, z_peers[i]],
            send_sem=pass_sem.at[mb, g, i, j],
            recv_sem=kv_sem.at[mb, g, z_peers[i]],
            device_id=(section, x_peers[j]),
            device_id_type=MESH,
        )

    def arrived(mb, g, slot):
        block = kv.at[mb, g, slot]
        pltpu.make_async_copy(block, block, kv_sem.at[mb, g, slot]).wait()

    def hand_on(mb, g):
        for i in range(z_size - 1):
            arrived(mb, g, z_peers[i])
            for j in range(x_size - 1):
                pass_copy(mb, g, i, j).start()

    def all_here(mb, g):
        for d in range(1, x_size):
            for e in range(z_size):
                arrived(mb, g, lax.rem(z + e, z_size) * x_size + lax.rem(x + d, x_size))

    def next_copy(mb, g):
        return pltpu.make_async_remote_copy(
            src_ref=result.at[mb, g],
            dst_ref=state.at[mb, g],
            send_sem=next_sem.at[mb, g],
            recv_sem=state_sem.at[mb, g],
            device_id=(section + 1, me),
            device_id_type=MESH,
        )

    def out_copy(mb, g):
        return pltpu.make_async_copy(
            result.at[mb, g],
            out_ref.at[0, mb, :, pl.ds(pl.multiple_of(g * chunk, chunk), chunk)],
            out_sem.at[mb, g],
        )

    def turn_queries(mb):
        raw_copy(mb).wait()
        spread = cosine[mb] * fold
        cross = sine[mb] * fold

        def group(g, carry):
            for r in range(RATIO):
                h = g * RATIO + r
                query = raw[mb, :, pl.ds(pl.multiple_of(h * HD, HD), HD)].astype(jnp.float32)
                turned[mb, h] = (query * spread + pltpu.roll(query, HD // 2, 1) * cross).astype(
                    jnp.bfloat16
                )
            return carry

        lax.fori_loop(0, HK, group, 0)

    def attend(mb):
        hand_on(mb, 0)

        def group(g, carry):
            @pl.when(g < HK - 1)
            def _():
                hand_on(mb, g + 1)

            all_here(mb, g)
            values[:, :HD] = kv[mb, g, :, :, HD:].reshape(seq_len, HD)
            for t in range(RATIO // TILE_HEADS):
                query = turned[mb, pl.ds(g * RATIO + t * TILE_HEADS, TILE_HEADS)]
                keys = kv[mb, g, :, :, :HD].reshape(seq_len, HD)
                scores = lax.dot_general(
                    query.reshape(TILE_HEADS * rows, HD),
                    keys,
                    (((1,), (1,)), ((), ())),
                    preferred_element_type=jnp.float32,
                )
                scores = scores.reshape(TILE_HEADS, rows, seq_len) + bias[mb]
                top = jnp.max(scores, axis=-1, keepdims=True)
                weights = jnp.exp2(scores - top).astype(jnp.bfloat16)
                summed = jnp.dot(
                    weights.reshape(TILE_HEADS * rows, seq_len),
                    values[...],
                    preferred_element_type=jnp.float32,
                )
                attended = (summed[:, :HD] / summed[:, HD:]).astype(jnp.bfloat16)
                for r in range(TILE_HEADS):
                    part = pl.ds((t * TILE_HEADS + r) * HD, HD)
                    result[mb, g, :, part] = (
                        state[mb, g, :, part].astype(jnp.float32)
                        + attended[r * rows : (r + 1) * rows].astype(jnp.float32)
                    ).astype(jnp.bfloat16)

            @pl.when(section < sections - 1)
            def _():
                next_copy(mb, g).start()

            out_copy(mb, g).start()
            return carry

        lax.fori_loop(0, HK, group, 0)

    prepare(0)

    @pl.when(section > 0)
    def _():
        for mb in range(1, micro):
            prepare(mb)
        for mb in range(micro):
            turn_queries(mb)

    project(0, True)

    @pl.when(section == 0)
    def _():
        for mb in range(1, micro):
            prepare(mb)
            project(mb, False)
        for mb in range(micro):
            turn_queries(mb)

    for mb in range(micro):
        attend(mb)
        if mb + 1 < micro:

            @pl.when(section > 0)
            def _():
                project(mb + 1, False)

    def finish(g, carry):
        for mb in range(micro):
            for i in range(len(z_peers) + len(x_peers)):
                own_copy(mb, g, i).wait_send()
            for i in range(z_size - 1):
                for j in range(x_size - 1):
                    pass_copy(mb, g, i, j).wait_send()
            out_copy(mb, g).wait()

            @pl.when(section < sections - 1)
            def _():
                next_copy(mb, g).wait_send()

        return carry

    lax.fori_loop(0, HK, finish, 0)


def local(sections, z_size, x_size, hidden, queries, gain, key_weight, value_weight, tree_ids,
          branch_ids, span_order):
    micro, rows, width = hidden.shape
    seq_len = tree_ids.shape[1]
    seq = z_size * x_size
    chunk = width // HK
    within = jnp.arange(SPAN, dtype=jnp.int32)
    packed = (span_order[:, :, None] * SPAN + within).reshape(micro, seq_len)
    exponent = np.arange(HD // 2, dtype=np.float32) * np.float32(2.0 / HD)
    inverse = np.power(np.float32(ROPE_BASE), -exponent).astype(np.float32)
    inverse = jnp.asarray(np.concatenate([inverse, inverse])[None])
    vmem = pl.BlockSpec(memory_space=pltpu.VMEM)
    anywhere = pl.BlockSpec(memory_space=pl.ANY)
    half = jnp.bfloat16
    dma = pltpu.SemaphoreType.DMA
    return pl.pallas_call(
        functools.partial(kernel, sections, z_size, x_size),
        out_shape=jax.ShapeDtypeStruct((1, micro, rows, width), half),
        in_specs=[pl.BlockSpec(memory_space=pltpu.SMEM)] + [vmem] * 5 + [anywhere] * 4,
        out_specs=anywhere,
        scratch_shapes=[
            pltpu.VMEM((micro, HK, rows, chunk), half),
            pltpu.VMEM((micro, rows, width), half),
            pltpu.VMEM((micro, HQ, rows, HD), half),
            pltpu.VMEM((width, HK * HD), half),
            pltpu.VMEM((width, HK * HD), half),
            pltpu.VMEM((2, rows, HK * HD), jnp.float32),
            pltpu.VMEM((micro, rows, HD), jnp.float32),
            pltpu.VMEM((micro, rows, HD), jnp.float32),
            pltpu.VMEM((micro, rows, seq_len), jnp.float32),
            pltpu.VMEM((micro, HK, seq, rows, 2 * HD), half),
            pltpu.VMEM((seq_len, 2 * HD), half),
            pltpu.VMEM((micro, HK, rows, chunk), half),
            dma((micro, HK)),
            dma((micro,)),
            dma((2, HK)),
            dma((micro, HK)),
            dma((micro, HK)),
            dma((micro, HK, z_size + x_size - 2)),
            dma((micro, HK, max(z_size - 1, 1), max(x_size - 1, 1))),
            dma((micro, HK, seq)),
        ],
        compiler_params=pltpu.CompilerParams(
            collective_id=0, has_side_effects=True, vmem_limit_bytes=56 * 1024 * 1024
        ),
    )(span_order, tree_ids, branch_ids, packed, inverse, gain, hidden, queries, key_weight, value_weight)


def solution(mesh):
    seq = mesh.shape["seq"]
    z_size = math.gcd(seq, 4)
    placed = (
        P(None, "seq", None),
        P("section", None, "seq", None),
        P("section", None),
        P("section", None, None),
        P("section", None, None),
        P(),
        P(),
        P(),
    )
    return jax.shard_map(
        functools.partial(local, mesh.shape["section"], z_size, seq // z_size),
        mesh=mesh,
        in_specs=placed,
        out_specs=P("section", None, "seq", None),
        check_vma=False,
    )
```
